128 devices in a mesh: face: 8 (over z_lo, x), sub: 16 (over y, z_hi, core).
Axes of the slice: x: 4, y: 4, z: 4 (z_hi: 2, z_lo: 2; z = z_hi * 2 + z_lo), core: 2. Of those that a mesh axis runs over, the one named last changes fastest.
Arguments:
- tokens: bfloat16 [131072, 1024], P(('face', 'sub')), may hold values from -6 to 6
- w_qkv: bfloat16 [1024, 3072], replicated
- w_out: bfloat16 [1024, 1024], replicated, may hold values from -0.1875 to 0.1875
- neighbours: int32 [2048, 9], P(('face', 'sub')), may hold values from 0 to 2047, as said below
- parent_one: int32 [131072], P(('face', 'sub')), may hold values from 0 to 127, as said below
- parent_two: int32 [128], replicated, may hold values from 0 to 31, as said below
- level_bias: float32 [2, 16], replicated, may hold values from -2 to 0
Outputs:
- mixed: bfloat16 [131072, 1024], P(('face', 'sub'))
The draws below stay inside these ranges and needn't reach their ends.
Inputs may be any that keep to these rules, and one draw needn't show every extreme that they name: Fine blocks lie on a periodic grid of 2 * 8 rows by 8 * 16 columns; block id = device * 16 + r * 8 + c, device = face index * 16 + sub index. Each row lists the block and its eight neighbours on that grid in row-major order, except that in some rows one diagonal neighbour is replaced by the block itself. `parent_one`: every token of a fine block has the same first-level cell, and the 16 blocks of each aligned 4 x 4 square of the block grid share one; each cell has 1024 tokens. `parent_two`: the four first-level cells of each aligned 2 x 2 square of cells share one second-level cell.
All inputs are finite; a program needn't handle non-finite values.
Results may differ from the reference program's by a relative error of at most 0.014.
Values may be sent and summed in bfloat16 or wider, within the bound.
A program may use at most 256 MiB of HBM per device.

```python
import jax
import jax.numpy as jnp
from jax import lax

D = 1024
HEADS = 16
HD = 64
BT = 64
BR = 2
BC = 8
BLK = 16
TOKENS = 131072
NB = 2048
NC1 = 128
NC2 = 32
N_FACE = 8
N_SUB = 16


def block_place(block_ids):
    owner = block_ids // BLK
    local = block_ids % BLK
    grow = owner // N_SUB * BR + local // BC
    gcol = owner % N_SUB * BC + local % BC
    return (grow, gcol)


def coarse_labels(key):
    perm_one = jax.random.permutation(jax.random.fold_in(key, 11), NC1).astype(jnp.int32)
    perm_two = jax.random.permutation(jax.random.fold_in(key, 12), NC2).astype(jnp.int32)
    return (perm_one, perm_two)


def draw_tokens(key, part):
    return jax.random.truncated_normal(jax.random.fold_in(key, 51), -6.0, 6.0, (TOKENS, D), jnp.float32).astype(jnp.bfloat16)


def draw_w_qkv(key, part):
    base = jax.random.truncated_normal(jax.random.fold_in(key, 61), -6.0, 6.0, (D, 3 * D), jnp.float32) * D ** (-0.5)
    return base.astype(jnp.bfloat16)


def draw_neighbours(key, part):
    grid_rows = BR * N_FACE
    grid_cols = BC * N_SUB
    block_ids = jnp.arange(NB, dtype=jnp.int32)
    grow, gcol = block_place(block_ids)
    step_r = jnp.array([-1, -1, -1, 0, 0, 0, 1, 1, 1], jnp.int32)
    step_c = jnp.array([-1, 0, 1, -1, 0, 1, -1, 0, 1], jnp.int32)
    near_r = (grow[:, None] + step_r[None, :]) % grid_rows
    near_c = (gcol[:, None] + step_c[None, :]) % grid_cols
    owner = near_r // BR * N_SUB + near_c // BC
    ids = owner * BLK + near_r % BR * BC + near_c % BC
    flagged = jax.random.randint(jax.random.fold_in(key, 21), (NB,), 0, 4) == 0
    corners = jnp.array([0, 2, 6, 8], jnp.int32)
    pick = corners[jax.random.randint(jax.random.fold_in(key, 22), (NB,), 0, 4)]
    replace = (jnp.arange(9, dtype=jnp.int32)[None, :] == pick[:, None]) & flagged[:, None]
    return jnp.where(replace, block_ids[:, None], ids).astype(jnp.int32)


def draw_parent_one(key, part):
    perm_one, perm_two = coarse_labels(key)
    grow, gcol = block_place(jnp.arange(NB, dtype=jnp.int32))
    cell = grow // 4 * (BC * N_SUB // 4) + gcol // 4
    return jnp.repeat(perm_one[cell], BT).astype(jnp.int32)


def draw_parent_two(key, part):
    perm_one, perm_two = coarse_labels(key)
    cells = jnp.arange(NC1, dtype=jnp.int32)
    across = BC * N_SUB // 4
    upper = cells // across // 2 * (across // 2) + cells % across // 2
    return jnp.zeros((NC1,), jnp.int32).at[perm_one].set(perm_two[upper]).astype(jnp.int32)


def bell_draw(stream_key, dims, spread, bound, kind=jnp.bfloat16):
    values = spread * jax.random.normal(stream_key, dims, jnp.float32)
    return jnp.clip(values, min=-bound, max=bound).astype(kind)


def setup_inputs(seed: int = 0) -> dict:
    seeds = jax.random.split(jax.random.key(seed), 8)
    tokens = draw_tokens(jax.random.fold_in(seeds[7], 71), 0)
    w_qkv = draw_w_qkv(jax.random.fold_in(seeds[7], 71), 0)
    w_out = bell_draw(seeds[2], (D, D), D ** -0.5, 0.1875)
    neighbours = draw_neighbours(jax.random.fold_in(seeds[7], 71), 0)
    parent_one = draw_parent_one(jax.random.fold_in(seeds[7], 71), 0)
    parent_two = draw_parent_two(jax.random.fold_in(seeds[7], 71), 0)
    level_bias = jnp.clip(jax.random.uniform(seeds[6], (2, HEADS), jnp.float32, -2.0, 0.0), -2.0, 0.0)
    return dict(tokens=tokens, w_qkv=w_qkv, w_out=w_out, neighbours=neighbours, parent_one=parent_one, parent_two=parent_two, level_bias=level_bias)


def rms_rows(sums):
    count = sums.shape[0]
    grouped = sums.reshape(count, 2, HEADS, HD)
    grouped = grouped * lax.rsqrt(lax.optimization_barrier(jnp.mean(grouped * grouped, axis=-1, keepdims=True)) + 1e-05)
    return grouped.reshape(count, 2 * D).astype(jnp.bfloat16)

def reference(tokens, w_qkv, w_out, neighbours, parent_one, parent_two, level_bias):
    proj = jnp.dot(tokens, w_qkv, preferred_element_type=jnp.float32).astype(jnp.bfloat16)
    query = proj[:, :D]
    pairs = proj[:, D:]
    sums_one = jax.ops.segment_sum(pairs.astype(jnp.float32), parent_one, NC1)
    sums_two = jax.ops.segment_sum(sums_one, parent_two, NC2)
    far = jnp.concatenate([rms_rows(sums_one), rms_rows(sums_two)], axis=0)
    far_keys = far[:, :D].reshape(-1, HEADS, HD).astype(jnp.float32)
    far_vals = far[:, D:].reshape(-1, HEADS, HD).astype(jnp.float32)
    bias = jnp.concatenate([jnp.broadcast_to(level_bias[0], (NC1, HEADS)), jnp.broadcast_to(level_bias[1], (NC2, HEADS))], axis=0).T
    scale = HD ** (-0.5)
    block_pairs = pairs.reshape(NB, BT, 2 * D)
    q_groups = query.reshape(NB // 8, 8, BT, HEADS, HD)
    idx_groups = neighbours.reshape(NB // 8, 8, 9)

    def attend(args):
        qb, ib = args
        qf = qb.astype(jnp.float32)
        near = block_pairs[ib].reshape(8, 9 * BT, 2, HEADS, HD).astype(jnp.float32)
        s_near = jnp.einsum('bqhd,bkhd->bhqk', qf, near[:, :, 0]) * scale
        s_far = jnp.einsum('bqhd,khd->bhqk', qf, far_keys) * scale + bias[None, :, None, :]
        weights = jax.nn.softmax(jnp.concatenate([s_near, s_far], axis=-1), axis=-1).astype(jnp.bfloat16).astype(jnp.float32)
        out = jnp.einsum('bhqk,bkhd->bqhd', weights[..., :9 * BT], near[:, :, 1])
        out = out + jnp.einsum('bhqk,khd->bqhd', weights[..., 9 * BT:], far_vals)
        return out.astype(jnp.bfloat16).reshape(8 * BT, D)
    heard = lax.map(attend, (q_groups, idx_groups)).reshape(TOKENS, D)
    return jnp.dot(heard, w_out, preferred_element_type=jnp.float32).astype(jnp.bfloat16)
```

```python
import functools

import jax
import jax.numpy as jnp
from jax import lax
from jax.experimental import pallas as pl
from jax.experimental.pallas import tpu as pltpu
from jax.sharding import PartitionSpec as P

D = 1024
HEADS = 16
HD = 64
BT = 64
BR = 2
BC = 8
GROUP = 4
GW = GROUP * HD
WIDE = BC + 2
EXT_ROW = WIDE * BT
EXT = (BR + 2) * EXT_ROW
ROW = BC * BT
LOG2E = 1.4426950408889634
MESH = pl.DeviceIdType.MESH
BF = jnp.bfloat16
F32 = jnp.float32


def kernel(
    n_face,
    n_sub,
    x_ref,
    wqkv_ref,
    wout_ref,
    near_ref,
    bias_ref,
    out_ref,
    xe,
    wq,
    wo,
    q,
    kv,
    heard,
    mixed,
    part,
    cells,
    far,
    load_sem,
    store_sem,
    halo_send,
    halo_recv,
    part_send,
    part_recv,
    cell_send,
    cell_recv,
):
    face = lax.axis_index("face")
    sub = lax.axis_index("sub")
    up = lax.rem(face + n_face - 1, n_face)
    down = lax.rem(face + 1, n_face)
    left = lax.rem(sub + n_sub - 1, n_sub)
    right = lax.rem(sub + 1, n_sub)
    n_one = n_sub * 8
    n_two = n_sub * 2
    n_far = n_one + n_two

    peers = [(lax.rem(face + d, n_face), sub) for d in range(1, n_face)]
    peers += [(face, lax.rem(sub + d, n_sub)) for d in range(1, n_sub)]
    peers += [(up, left), (up, right), (down, left), (down, right)]
    barrier = pltpu.get_barrier_semaphore()
    for peer in peers:
        pl.semaphore_signal(barrier, inc=1, device_id=peer, device_id_type=MESH)

    own = [(EXT_ROW + BT, 0), (2 * EXT_ROW + BT, ROW)]
    loads = []
    for i, (to, at) in enumerate(own):
        loads.append(
            pltpu.make_async_copy(
                x_ref.at[pl.ds(at, ROW)], xe.at[pl.ds(to, ROW)], load_sem.at[i]
            )
        )
    loads.append(pltpu.make_async_copy(wqkv_ref, wq, load_sem.at[2]))
    loads.append(pltpu.make_async_copy(wout_ref, wo, load_sem.at[3]))
    for load in loads:
        load.start()

    pl.semaphore_wait(barrier, len(peers))

    last = ROW - BT
    sends = [
        (0, BT, 3 * EXT_ROW + 9 * BT, (up, left)),
        (last, BT, 3 * EXT_ROW, (up, right)),
        (ROW, BT, 9 * BT, (down, left)),
        (ROW + last, BT, 0, (down, right)),
        (0, ROW, 3 * EXT_ROW + BT, (up, sub)),
        (ROW, ROW, BT, (down, sub)),
        (0, BT, EXT_ROW + 9 * BT, (face, left)),
        (ROW, BT, 2 * EXT_ROW + 9 * BT, (face, left)),
        (last, BT, EXT_ROW, (face, right)),
        (ROW + last, BT, 2 * EXT_ROW, (face, right)),
    ]
    halos = []
    for i, (at, rows, to, peer) in enumerate(sends):
        halos.append(
            pltpu.make_async_remote_copy(
                src_ref=x_ref.at[pl.ds(at, rows)],
                dst_ref=xe.at[pl.ds(to, rows)],
                send_sem=halo_send.at[i],
                recv_sem=halo_recv.at[i],
                device_id=peer,
                device_id_type=MESH,
            )
        )
    for halo in halos:
        halo.start()

    loads[0].wait()
    loads[1].wait()
    for half in range(2):
        total = None
        for to, _ in own:
            tok = xe[pl.ds(to + half * (ROW // 2), ROW // 2), :].astype(F32)
            s = jnp.sum(tok, axis=0, keepdims=True)
            total = s if total is None else total + s
        part[face, pl.ds(half, 1), :] = total
    parts = []
    for d in range(1, n_face):
        parts.append(
            pltpu.make_async_remote_copy(
                src_ref=part.at[face],
                dst_ref=part.at[face],
                send_sem=part_send.at[d],
                recv_sem=part_recv.at[d],
                device_id=(lax.rem(face + d, n_face), sub),
                device_id_type=MESH,
            )
        )
    for copy in parts:
        copy.start()

    loads[2].wait()

    def own_query(n, carry):
        cols = pl.ds(pl.multiple_of(n * GW, GW), GW)
        for to, at in own:
            y = jnp.dot(xe[pl.ds(to, ROW), :], wq[:, cols], preferred_element_type=F32)
            q[pl.ds(at, ROW), cols] = (y * (HD**-0.5 * LOG2E)).astype(BF)
        return carry

    lax.fori_loop(0, D // GW, own_query, 0)

    for copy in parts:
        copy.wait()
    for k in range(n_face // 2):
        cells[sub, pl.ds(2 * k, 2), :] = part[2 * k] + part[2 * k + 1]
    gathers = []
    for d in range(1, n_sub):
        gathers.append(
            pltpu.make_async_remote_copy(
                src_ref=cells.at[sub],
                dst_ref=cells.at[sub],
                send_sem=cell_send.at[d],
                recv_sem=cell_recv.at[d],
                device_id=(face, lax.rem(sub + d, n_sub)),
                device_id_type=MESH,
            )
        )
    for copy in gathers:
        copy.start()

    def pairs_of(start, rows):
        def step(n, carry):
            cols = pl.ds(pl.multiple_of(n * GW, GW), GW)
            wcols = pl.ds(pl.multiple_of(D + n * GW, GW), GW)
            y = jnp.dot(xe[pl.ds(start, rows), :], wq[:, wcols], preferred_element_type=F32)
            kv[pl.ds(start, rows), cols] = y.astype(BF)
            return carry

        lax.fori_loop(0, 2 * D // GW, step, 0)

    for to, _ in own:
        pairs_of(to, ROW)

    for copy in gathers:
        copy.wait()

    one = cells[...].reshape(n_one, D)
    one_hi = one.astype(BF)
    one_lo = (one - one_hi.astype(F32)).astype(BF)
    pick = (
        lax.broadcasted_iota(jnp.int32, (n_two, n_one), 1) // 4
        == lax.broadcasted_iota(jnp.int32, (n_two, n_one), 0)
    ).astype(BF)
    two = jnp.dot(pick, one_hi, preferred_element_type=F32) + jnp.dot(
        pick, one_lo, preferred_element_type=F32
    )
    two_hi = two.astype(BF)
    two_lo = (two - two_hi.astype(F32)).astype(BF)
    sums = jnp.concatenate([one_hi, two_hi, one_lo, two_lo], axis=0)
    same = (
        lax.broadcasted_iota(jnp.int32, (GW, GW), 0) // HD
        == lax.broadcasted_iota(jnp.int32, (GW, GW), 1) // HD
    )
    mean = jnp.where(same, 1.0 / HD, 0.0).astype(BF)

    def pooled(n, carry):
        cols = pl.ds(pl.multiple_of(n * GW, GW), GW)
        wcols = pl.ds(pl.multiple_of(D + n * GW, GW), GW)
        y = jnp.dot(sums, wq[:, wcols], preferred_element_type=F32)
        y = y[:n_far] + y[n_far:]
        sq = jnp.dot((y * y).astype(BF), mean, preferred_element_type=F32)
        far[:, cols] = (y * lax.rsqrt(sq + 1e-5)).astype(BF)
        return carry

    lax.fori_loop(0, 2 * D // GW, pooled, 0)

    for halo in halos:
        halo.wait()
    pairs_of(0, EXT_ROW + BT)
    pairs_of(2 * EXT_ROW - BT, 2 * BT)
    pairs_of(3 * EXT_ROW - BT, EXT_ROW + BT)

    lane = lax.broadcasted_iota(jnp.int32, (BT, GW), 1) // HD
    lane_far = lax.broadcasted_iota(jnp.int32, (BT, 128), 1)

    def attend(b, carry):
        corner = b // BC * EXT_ROW + b % BC * BT
        me = corner + EXT_ROW + BT
        own_id = near_ref[b, 4]
        starts = []
        for j in range(9):
            at = corner + j // 3 * EXT_ROW + j % 3 * BT
            if j in (0, 2, 6, 8):
                other = near_ref[b, j] - own_id
                at = me + (at - me) * jnp.minimum(other * other, 1)
            starts.append(at)
        rows = pl.ds(pl.multiple_of(b * BT, BT), BT)
        for g in range(HEADS // GROUP):
            cols = pl.ds(g * GW, GW)
            vcols = pl.ds(D + g * GW, GW)
            qb = q[rows, cols]
            zero = jnp.zeros_like(qb)
            qs = jnp.concatenate([jnp.where(lane == h, qb, zero) for h in range(GROUP)], axis=0)
            keys = jnp.concatenate(
                [far[:, cols]] + [kv[pl.ds(at, BT), cols] for at in starts], axis=0
            )
            vals = jnp.concatenate(
                [far[:, vcols]] + [kv[pl.ds(at, BT), vcols] for at in starts], axis=0
            )
            s = lax.dot_general(
                qs, keys, (((1,), (1,)), ((), ())), preferred_element_type=F32
            )
            add_one = jnp.concatenate(
                [jnp.full((BT, 128), bias_ref[0, g * GROUP + h] * LOG2E, F32) for h in range(GROUP)],
                axis=0,
            )
            add_two = jnp.concatenate(
                [
                    jnp.where(lane_far < n_two, bias_ref[1, g * GROUP + h] * LOG2E, 0.0)
                    for h in range(GROUP)
                ],
                axis=0,
            )
            s = jnp.concatenate(
                [s[:, :128] + add_one, s[:, 128:256] + add_two, s[:, 256:]], axis=1
            )
            p = jnp.exp2(s - jnp.max(s, axis=1, keepdims=True))
            total = jnp.sum(p, axis=1, keepdims=True)
            o = jnp.dot(p.astype(BF), vals, preferred_element_type=F32)
            o = o * (1.0 / total)
            h01 = jnp.where(lane == 0, o[:BT], o[BT : 2 * BT])
            h23 = jnp.where(lane == 2, o[2 * BT : 3 * BT], o[3 * BT :])
            heard[rows, cols] = jnp.where(lane < 2, h01, h23).astype(BF)
        return carry

    lax.fori_loop(0, BR * BC, attend, 0)

    loads[3].wait()

    def project(n, carry):
        cols = pl.ds(pl.multiple_of(n * GW, GW), GW)
        y = jnp.dot(heard[...], wo[:, cols], preferred_element_type=F32)
        mixed[:, cols] = y.astype(BF)
        return carry

    lax.fori_loop(0, D // GW, project, 0)
    store = pltpu.make_async_copy(mixed, out_ref, store_sem)
    store.start()
    store.wait()


def solution(mesh):
    n_face, n_sub = mesh.shape["face"], mesh.shape["sub"]
    tokens = BR * ROW
    n_far = n_sub * 10

    def body(x, w_qkv, w_out, neighbours, parent_one, parent_two, level_bias):
        call = pl.pallas_call(
            functools.partial(kernel, n_face, n_sub),
            out_shape=jax.ShapeDtypeStruct((tokens, D), BF),
            in_specs=[pl.BlockSpec(memory_space=pl.ANY)] * 3
            + [pl.BlockSpec(memory_space=pltpu.SMEM)] * 2,
            out_specs=pl.BlockSpec(memory_space=pl.ANY),
            scratch_shapes=[
                pltpu.VMEM((EXT, D), BF),
                pltpu.VMEM((D, 3 * D), BF),
                pltpu.VMEM((D, D), BF),
                pltpu.VMEM((tokens, D), BF),
                pltpu.VMEM((EXT, 2 * D), BF),
                pltpu.VMEM((tokens, D), BF),
                pltpu.VMEM((tokens, D), BF),
                pltpu.VMEM((n_face, 2, D), F32),
                pltpu.VMEM((n_sub, 8, D), F32),
                pltpu.VMEM((n_far, 2 * D), BF),
                pltpu.SemaphoreType.DMA((4,)),
                pltpu.SemaphoreType.DMA,
                pltpu.SemaphoreType.DMA((10,)),
                pltpu.SemaphoreType.DMA((10,)),
                pltpu.SemaphoreType.DMA((n_face,)),
                pltpu.SemaphoreType.DMA((n_face,)),
                pltpu.SemaphoreType.DMA((n_sub,)),
                pltpu.SemaphoreType.DMA((n_sub,)),
            ],
            compiler_params=pltpu.CompilerParams(
                collective_id=0, has_side_effects=True, vmem_limit_bytes=56 * 1024 * 1024
            ),
            cost_estimate=pl.CostEstimate(
                flops=60_000_000_000, bytes_accessed=16_000_000, transcendentals=12_000_000
            ),
        )
        return call(x, w_qkv, w_out, neighbours, level_bias)

    placed = (
        P(("face", "sub"), None),
        P(),
        P(),
        P(("face", "sub"), None),
        P(("face", "sub")),
        P(),
        P(),
    )
    return jax.shard_map(
        body, mesh=mesh, in_specs=placed, out_specs=P(("face", "sub"), None), check_vma=False
    )
```

```python
import functools

import jax
import jax.numpy as jnp
from jax import lax
from jax.experimental import pallas as pl
from jax.experimental.pallas import tpu as pltpu
from jax.sharding import PartitionSpec as P

D = 1024
HEADS = 16
HD = 64
BT = 64
BR = 2
BC = 8
GROUP = 4
GW = GROUP * HD
WIDE = BC + 2
EXT_ROW = WIDE * BT
EXT = (BR + 2) * EXT_ROW
ROW = BC * BT
LOG2E = 1.4426950408889634
MESH = pl.DeviceIdType.MESH
BF = jnp.bfloat16
F32 = jnp.float32


def kernel(
    n_face,
    n_sub,
    x_ref,
    wqkv_ref,
    wout_ref,
    near_ref,
    bias_ref,
    out_ref,
    xe,
    wq,
    wo,
    q,
    kv,
    heard,
    mixed,
    part,
    cells,
    far,
    load_sem,
    store_sem,
    halo_send,
    halo_recv,
    part_send,
    part_recv,
    cell_send,
    cell_recv,
):
    face = lax.axis_index("face")
    sub = lax.axis_index("sub")
    up = lax.rem(face + n_face - 1, n_face)
    down = lax.rem(face + 1, n_face)
    left = lax.rem(sub + n_sub - 1, n_sub)
    right = lax.rem(sub + 1, n_sub)
    n_one = n_sub * 8
    n_two = n_sub * 2
    n_far = n_one + n_two

    core = lax.rem(sub, 2)
    high = lax.rem(sub // 2, 2)
    mate = sub + 1 - 2 * core
    across = sub + 2 - 4 * high
    along = [lax.rem(sub + d, n_sub) for d in range(4, n_sub, 4)]
    n_y = n_sub // 4
    shelf = core * (2 * n_y) + sub // 4 * 2
    slot = shelf + high

    peers = [(lax.rem(face + d, n_face), sub) for d in range(1, n_face)]
    peers += [(face, left), (face, right), (face, across)] + [(face, far_y) for far_y in along]
    barrier = pltpu.get_barrier_semaphore()
    for peer in peers:
        pl.semaphore_signal(barrier, inc=1, device_id=peer, device_id_type=MESH)

    own = [(EXT_ROW + BT, 0), (2 * EXT_ROW + BT, ROW)]
    loads = []
    for i, (to, at) in enumerate(own):
        loads.append(
            pltpu.make_async_copy(
                x_ref.at[pl.ds(at, ROW)], xe.at[pl.ds(to, ROW)], load_sem.at[i]
            )
        )
    for i in range(3):
        cols = pl.ds(i * D, D)
        loads.append(
            pltpu.make_async_copy(wqkv_ref.at[:, cols], wq.at[:, cols], load_sem.at[2 + i])
        )
    loads.append(pltpu.make_async_copy(wout_ref, wo, load_sem.at[5]))
    for load in loads:
        load.start()

    loads[0].wait()
    loads[1].wait()
    for half in range(2):
        total = None
        for to, _ in own:
            tok = xe[pl.ds(to + half * (ROW // 2), ROW // 2), :].astype(F32)
            s = jnp.sum(tok, axis=0, keepdims=True)
            total = s if total is None else total + s
        part[face, pl.ds(half, 1), :] = total

    def matmul(row_starts, rows, first, out, out_starts, out_first, width, scale):
        def step(n, carry):
            wcols = pl.ds(pl.multiple_of(first + n * width, width), width)
            cols = pl.ds(pl.multiple_of(out_first + n * width, width), width)
            x = [xe[pl.ds(at, rows), :] for at in row_starts]
            x = x[0] if len(x) == 1 else jnp.concatenate(x, axis=0)
            y = jnp.dot(x, wq[:, wcols], preferred_element_type=F32)
            if scale is not None:
                y = y * scale
            y = y.astype(BF)
            for i, at in enumerate(out_starts):
                out[pl.ds(at, rows), cols] = y[i * rows : (i + 1) * rows]
            return carry

        return step

    own_at = [to for to, _ in own]
    loads[2].wait()
    lax.fori_loop(
        0, 2, matmul(own_at, ROW, 0, q, [0, ROW], 0, 512, HD**-0.5 * LOG2E), 0
    )
    loads[3].wait()
    lax.fori_loop(0, 2, matmul(own_at, ROW, D, kv, own_at, 0, 512, None), 0)
    loads[4].wait()

    pl.semaphore_wait(barrier, len(peers))

    parts = []
    for d in range(1, n_face):
        parts.append(
            pltpu.make_async_remote_copy(
                src_ref=part.at[face],
                dst_ref=part.at[face],
                send_sem=part_send.at[d],
                recv_sem=part_recv.at[d],
                device_id=(lax.rem(face + d, n_face), sub),
                device_id_type=MESH,
            )
        )
    for copy in parts:
        copy.start()

    def remote(src, src_at, rows, to, peer, i):
        return pltpu.make_async_remote_copy(
            src_ref=src.at[pl.ds(src_at, rows)],
            dst_ref=xe.at[pl.ds(to, rows)],
            send_sem=halo_send.at[i],
            recv_sem=halo_recv.at[i],
            device_id=peer,
            device_id_type=MESH,
        )

    bottom = 3 * EXT_ROW
    last = ROW - BT
    edges = [
        remote(x_ref, 0, BT, bottom + BT, (up, sub), 0),
        remote(x_ref, ROW, BT, BT, (down, sub), 1),
        remote(x_ref, last, BT, bottom + BC * BT, (up, sub), 2),
        remote(x_ref, ROW + last, BT, BC * BT, (down, sub), 3),
    ]

    def chunk(k):
        at = BT + k * (2 * BT)
        return [
            remote(x_ref, at, 2 * BT, bottom + BT + at, (up, sub), 4 + 2 * k),
            remote(x_ref, ROW + at, 2 * BT, BT + at, (down, sub), 5 + 2 * k),
        ]

    sides = [
        remote(x_ref, last, BT, EXT_ROW, (face, right), 10),
        remote(x_ref, ROW + last, BT, 2 * EXT_ROW, (face, right), 11),
        remote(x_ref, 0, BT, EXT_ROW + 9 * BT, (face, left), 12),
        remote(x_ref, ROW, BT, 2 * EXT_ROW + 9 * BT, (face, left), 13),
    ]
    corners = [
        remote(xe, BC * BT, BT, 0, (face, right), 14),
        remote(xe, bottom + BC * BT, BT, bottom, (face, right), 15),
        remote(xe, BT, BT, 9 * BT, (face, left), 16),
        remote(xe, bottom + BT, BT, bottom + 9 * BT, (face, left), 17),
    ]
    for copy in edges + chunk(0):
        copy.start()

    lax.fori_loop(0, 2, matmul(own_at, ROW, 2 * D, kv, own_at, D, 512, None), 0)

    for copy in parts:
        copy.wait()
    for k in range(n_face // 2):
        cells[slot, pl.ds(2 * k, 2), :] = part[2 * k] + part[2 * k + 1]

    def gather(at, count, peer, i):
        return pltpu.make_async_remote_copy(
            src_ref=cells.at[pl.ds(at, count)],
            dst_ref=cells.at[pl.ds(at, count)],
            send_sem=cell_send.at[i],
            recv_sem=cell_recv.at[i],
            device_id=(face, peer),
            device_id_type=MESH,
        )

    gather_z = gather(slot, 1, across, 0)
    gather_y = [gather(shelf, 2, peer, 1 + i) for i, peer in enumerate(along)]
    gather_core = gather(core * (2 * n_y), 2 * n_y, mate, n_y)
    gather_z.start()
    gather_z.wait()
    for copy in gather_y:
        copy.start()
    for copy in chunk(1):
        copy.start()

    def project(starts):
        lax.fori_loop(0, 2, matmul(starts, BT, D, kv, starts, 0, D, None), 0)

    for copy in edges:
        copy.wait_recv()
    for copy in corners:
        copy.start()
    project([BT, BC * BT, bottom + BT, bottom + BC * BT])

    for copy in gather_y:
        copy.wait()
    gather_core.start()
    for copy in chunk(2):
        copy.start()
    gather_core.wait()
    for copy in sides:
        copy.start()

    one = cells[...].reshape(n_one, D)
    one_hi = one.astype(BF)
    one_lo = (one - one_hi.astype(F32)).astype(BF)
    pick = (
        lax.broadcasted_iota(jnp.int32, (n_two, n_one), 1) // 4
        == lax.broadcasted_iota(jnp.int32, (n_two, n_one), 0)
    ).astype(BF)
    two = jnp.dot(pick, one_hi, preferred_element_type=F32) + jnp.dot(
        pick, one_lo, preferred_element_type=F32
    )
    two_hi = two.astype(BF)
    two_lo = (two - two_hi.astype(F32)).astype(BF)
    sums = jnp.concatenate([one_hi, two_hi, one_lo, two_lo], axis=0)
    same = (
        lax.broadcasted_iota(jnp.int32, (GW, GW), 0) // HD
        == lax.broadcasted_iota(jnp.int32, (GW, GW), 1) // HD
    )
    mean = jnp.where(same, 1.0 / HD, 0.0).astype(BF)

    def pooled(n, carry):
        cols = pl.ds(pl.multiple_of(n * GW, GW), GW)
        wcols = pl.ds(pl.multiple_of(D + n * GW, GW), GW)
        y = jnp.dot(sums, wq[:, wcols], preferred_element_type=F32)
        y = y[:n_far] + y[n_far:]
        sq = jnp.dot((y * y).astype(BF), mean, preferred_element_type=F32)
        far[:, cols] = (y * lax.rsqrt(sq + 1e-5)).astype(BF)
        return carry

    lax.fori_loop(0, 2 * D // GW, pooled, 0)

    lane = lax.broadcasted_iota(jnp.int32, (BT, GW), 1) // HD
    lane_far = lax.broadcasted_iota(jnp.int32, (BT, 128), 1)

    def attend(c):
        items = []
        for r in range(BR):
            corner = r * EXT_ROW + c * BT
            me = corner + EXT_ROW + BT
            b = r * BC + c
            own_id = near_ref[b, 4]
            starts = []
            for j in range(9):
                at = corner + j // 3 * EXT_ROW + j % 3 * BT
                if j in (0, 2, 6, 8):
                    other = near_ref[b, j] - own_id
                    at = me + (at - me) * jnp.minimum(other * other, 1)
                starts.append(at)
            rows = pl.ds(pl.multiple_of(b * BT, BT), BT)
            items += [(rows, starts, g) for g in range(HEADS // GROUP)]

        def scores(rows, starts, g):
            cols = pl.ds(g * GW, GW)
            qb = q[rows, cols]
            zero = jnp.zeros_like(qb)
            qs = jnp.concatenate([jnp.where(lane == h, qb, zero) for h in range(GROUP)], axis=0)
            keys = jnp.concatenate(
                [far[:, cols]] + [kv[pl.ds(at, BT), cols] for at in starts], axis=0
            )
            return lax.dot_general(
                qs, keys, (((1,), (1,)), ((), ())), preferred_element_type=F32
            )

        s_next = scores(*items[0])
        for i, (rows, starts, g) in enumerate(items):
            s = s_next
            if i + 1 < len(items):
                s_next = scores(*items[i + 1])
            add_one = jnp.concatenate(
                [jnp.full((BT, 128), bias_ref[0, g * GROUP + h] * LOG2E, F32) for h in range(GROUP)],
                axis=0,
            )
            add_two = jnp.concatenate(
                [
                    jnp.where(lane_far < n_two, bias_ref[1, g * GROUP + h] * LOG2E, 0.0)
                    for h in range(GROUP)
                ],
                axis=0,
            )
            s = jnp.concatenate(
                [s[:, :128] + add_one, s[:, 128:256] + add_two, s[:, 256:]], axis=1
            )
            p = jnp.exp2(s - jnp.max(s, axis=1, keepdims=True))
            total = jnp.sum(p, axis=1, keepdims=True)
            vcols = pl.ds(D + g * GW, GW)
            vals = jnp.concatenate(
                [far[:, vcols]] + [kv[pl.ds(at, BT), vcols] for at in starts], axis=0
            )
            o = jnp.dot(p.astype(BF), vals, preferred_element_type=F32)
            o = o * (1.0 / total)
            h01 = jnp.where(lane == 0, o[:BT], o[BT : 2 * BT])
            h23 = jnp.where(lane == 2, o[2 * BT : 3 * BT], o[3 * BT :])
            heard[rows, pl.ds(g * GW, GW)] = jnp.where(lane < 2, h01, h23).astype(BF)

    def middle(k, carry):
        for copy in chunk(k):
            copy.wait_recv()
        at = 2 * BT + k * (2 * BT)
        project([at, at + BT, bottom + at, bottom + at + BT])

        def column(c, carry):
            attend(c)
            return carry

        lax.fori_loop(1 + k * (k + 1) // 2, 1 + (k + 1) * (k + 2) // 2, column, 0)
        return carry

    lax.fori_loop(0, 3, middle, 0)

    for copy in sides + corners:
        copy.wait_recv()

    def outer(i, carry):
        at = i * (9 * BT)
        project([at, EXT_ROW + at, 2 * EXT_ROW + at, bottom + at])
        attend(i * (BC - 1))
        return carry

    lax.fori_loop(0, 2, outer, 0)

    loads[5].wait()
    stores = []
    for i in range(BR):
        rows = pl.ds(i * ROW, ROW)
        y = jnp.dot(heard[rows, :], wo[...], preferred_element_type=F32)
        mixed[rows, :] = y.astype(BF)
        store = pltpu.make_async_copy(mixed.at[rows], out_ref.at[rows], store_sem.at[i])
        store.start()
        stores.append(store)
    for copy in edges + chunk(0) + chunk(1) + chunk(2) + sides + corners:
        copy.wait_send()
    for store in stores:
        store.wait()


def solution(mesh):
    n_face, n_sub = mesh.shape["face"], mesh.shape["sub"]
    tokens = BR * ROW
    n_far = n_sub * 10

    def body(x, w_qkv, w_out, neighbours, parent_one, parent_two, level_bias):
        call = pl.pallas_call(
            functools.partial(kernel, n_face, n_sub),
            out_shape=jax.ShapeDtypeStruct((tokens, D), BF),
            in_specs=[pl.BlockSpec(memory_space=pl.ANY)] * 3
            + [pl.BlockSpec(memory_space=pltpu.SMEM)] * 2,
            out_specs=pl.BlockSpec(memory_space=pl.ANY),
            scratch_shapes=[
                pltpu.VMEM((EXT, D), BF),
                pltpu.VMEM((D, 3 * D), BF),
                pltpu.VMEM((D, D), BF),
                pltpu.VMEM((tokens, D), BF),
                pltpu.VMEM((EXT, 2 * D), BF),
                pltpu.VMEM((tokens, D), BF),
                pltpu.VMEM((tokens, D), BF),
                pltpu.VMEM((n_face, 2, D), F32),
                pltpu.VMEM((n_sub, 8, D), F32),
                pltpu.VMEM((n_far, 2 * D), BF),
                pltpu.SemaphoreType.DMA((6,)),
                pltpu.SemaphoreType.DMA((BR,)),
                pltpu.SemaphoreType.DMA((18,)),
                pltpu.SemaphoreType.DMA((18,)),
                pltpu.SemaphoreType.DMA((n_face,)),
                pltpu.SemaphoreType.DMA((n_face,)),
                pltpu.SemaphoreType.DMA((n_sub,)),
                pltpu.SemaphoreType.DMA((n_sub,)),
            ],
            compiler_params=pltpu.CompilerParams(
                collective_id=0, has_side_effects=True, vmem_limit_bytes=56 * 1024 * 1024
            ),
            cost_estimate=pl.CostEstimate(
                flops=60_000_000_000, bytes_accessed=16_000_000, transcendentals=12_000_000
            ),
        )
        return call(x, w_qkv, w_out, neighbours, level_bias)

    placed = (
        P(("face", "sub"), None),
        P(),
        P(),
        P(("face", "sub"), None),
        P(("face", "sub")),
        P(),
        P(),
    )
    return jax.shard_map(
        body, mesh=mesh, in_specs=placed, out_specs=P(("face", "sub"), None), check_vma=False
    )
```

```python
import functools

import jax
import jax.numpy as jnp
from jax import lax
from jax.experimental import pallas as pl
from jax.experimental.pallas import tpu as pltpu
from jax.sharding import PartitionSpec as P

D = 1024
HEADS = 16
HD = 64
BT = 64
BR = 2
BC = 8
GROUP = 4
GW = GROUP * HD
WIDE = BC + 2
EXT_ROW = WIDE * BT
EXT = (BR + 2) * EXT_ROW
ROW = BC * BT
LOG2E = 1.4426950408889634
MESH = pl.DeviceIdType.MESH
BF = jnp.bfloat16
F32 = jnp.float32


def kernel(
    n_face,
    n_sub,
    x_ref,
    wqkv_ref,
    wout_ref,
    near_ref,
    bias_ref,
    out_ref,
    xe,
    wq,
    wo,
    q,
    kv,
    heard,
    mixed,
    part,
    cells,
    far,
    load_sem,
    store_sem,
    halo_send,
    halo_recv,
    part_send,
    part_recv,
    cell_send,
    cell_recv,
):
    face = lax.axis_index("face")
    sub = lax.axis_index("sub")
    up = lax.rem(face + n_face - 1, n_face)
    down = lax.rem(face + 1, n_face)
    left = lax.rem(sub + n_sub - 1, n_sub)
    right = lax.rem(sub + 1, n_sub)
    n_one = n_sub * 8
    n_two = n_sub * 2
    n_far = n_one + n_two

    core = lax.rem(sub, 2)
    high = lax.rem(sub // 2, 2)
    mate = sub + 1 - 2 * core
    across = sub + 2 - 4 * high
    along = [lax.rem(sub + d, n_sub) for d in range(4, n_sub, 4)]
    n_y = n_sub // 4
    shelf = core * (2 * n_y) + sub // 4 * 2

    peers = [(lax.rem(face + d, n_face), sub) for d in range(1, n_face)]
    peers += [(lax.rem(face + d, n_face), across) for d in range(1, n_face)]
    peers += [(face, left), (face, right), (face, across)] + [(face, far_y) for far_y in along]
    barrier = pltpu.get_barrier_semaphore()
    for peer in peers:
        pl.semaphore_signal(barrier, inc=1, device_id=peer, device_id_type=MESH)

    own = [(EXT_ROW + BT, 0), (2 * EXT_ROW + BT, ROW)]
    loads = []
    for i, (to, at) in enumerate(own):
        loads.append(
            pltpu.make_async_copy(
                x_ref.at[pl.ds(at, ROW)], xe.at[pl.ds(to, ROW)], load_sem.at[i]
            )
        )
    for i in range(3):
        cols = pl.ds(i * D, D)
        loads.append(
            pltpu.make_async_copy(wqkv_ref.at[:, cols], wq.at[:, cols], load_sem.at[2 + i])
        )
    loads.append(pltpu.make_async_copy(wout_ref, wo, load_sem.at[5]))
    for load in loads:
        load.start()

    loads[0].wait()
    loads[1].wait()
    for half in range(2):
        total = None
        for to, _ in own:
            tok = xe[pl.ds(to + half * (ROW // 2), ROW // 2), :].astype(F32)
            s = jnp.sum(tok, axis=0, keepdims=True)
            total = s if total is None else total + s
        part[high * n_face + face, pl.ds(half, 1), :] = total

    def matmul(row_starts, rows, first, out, out_starts, out_first, width, scale):
        def step(n, carry):
            wcols = pl.ds(pl.multiple_of(first + n * width, width), width)
            cols = pl.ds(pl.multiple_of(out_first + n * width, width), width)
            x = [xe[pl.ds(at, rows), :] for at in row_starts]
            x = x[0] if len(x) == 1 else jnp.concatenate(x, axis=0)
            y = jnp.dot(x, wq[:, wcols], preferred_element_type=F32)
            if scale is not None:
                y = y * scale
            y = y.astype(BF)
            for i, at in enumerate(out_starts):
                out[pl.ds(at, rows), cols] = y[i * rows : (i + 1) * rows]
            return carry

        return step

    own_at = [to for to, _ in own]
    pl.semaphore_wait(barrier, len(peers))

    parts = []
    for d in range(1, 2 * n_face):
        parts.append(
            pltpu.make_async_remote_copy(
                src_ref=part.at[high * n_face + face],
                dst_ref=part.at[high * n_face + face],
                send_sem=part_send.at[d],
                recv_sem=part_recv.at[d],
                device_id=(lax.rem(face + d, n_face), sub if d < n_face else across),
                device_id_type=MESH,
            )
        )
    for copy in parts:
        copy.start()

    def remote(src, src_at, rows, to, peer, i):
        return pltpu.make_async_remote_copy(
            src_ref=src.at[pl.ds(src_at, rows)],
            dst_ref=xe.at[pl.ds(to, rows)],
            send_sem=halo_send.at[i],
            recv_sem=halo_recv.at[i],
            device_id=peer,
            device_id_type=MESH,
        )

    bottom = 3 * EXT_ROW
    last = ROW - BT
    edges = [
        remote(x_ref, 0, BT, bottom + BT, (up, sub), 0),
        remote(x_ref, ROW, BT, BT, (down, sub), 1),
        remote(x_ref, last, BT, bottom + BC * BT, (up, sub), 2),
        remote(x_ref, ROW + last, BT, BC * BT, (down, sub), 3),
    ]

    def chunk(k):
        at = BT + k * (2 * BT)
        return [
            remote(x_ref, at, 2 * BT, bottom + BT + at, (up, sub), 4 + 2 * k),
            remote(x_ref, ROW + at, 2 * BT, BT + at, (down, sub), 5 + 2 * k),
        ]

    def half(k, i):
        at = BT + k * (2 * BT) + i * BT
        return [
            remote(x_ref, at, BT, bottom + BT + at, (up, sub), 4 + 2 * k),
            remote(x_ref, ROW + at, BT, BT + at, (down, sub), 5 + 2 * k),
        ]

    sides = [
        remote(x_ref, last, BT, EXT_ROW, (face, right), 10),
        remote(x_ref, ROW + last, BT, 2 * EXT_ROW, (face, right), 11),
        remote(x_ref, 0, BT, EXT_ROW + 9 * BT, (face, left), 12),
        remote(x_ref, ROW, BT, 2 * EXT_ROW + 9 * BT, (face, left), 13),
    ]
    corners = [
        remote(xe, BC * BT, BT, 0, (face, right), 14),
        remote(xe, bottom + BC * BT, BT, bottom, (face, right), 15),
        remote(xe, BT, BT, 9 * BT, (face, left), 16),
        remote(xe, bottom + BT, BT, bottom + 9 * BT, (face, left), 17),
    ]
    for copy in edges[:2]:
        copy.start()

    loads[2].wait()
    lax.fori_loop(
        0, 2, matmul(own_at, ROW, 0, q, [0, ROW], 0, 512, HD**-0.5 * LOG2E), 0
    )
    loads[3].wait()
    lax.fori_loop(0, 2, matmul(own_at, ROW, D, kv, own_at, 0, 512, None), 0)

    for copy in parts:
        copy.wait()
    for h in range(2):
        for k in range(n_face // 2):
            pair = part[h * n_face + 2 * k] + part[h * n_face + 2 * k + 1]
            cells[shelf + h, pl.ds(2 * k, 2), :] = pair

    def gather(at, count, peer, i):
        return pltpu.make_async_remote_copy(
            src_ref=cells.at[pl.ds(at, count)],
            dst_ref=cells.at[pl.ds(at, count)],
            send_sem=cell_send.at[i],
            recv_sem=cell_recv.at[i],
            device_id=(face, peer),
            device_id_type=MESH,
        )

    gather_y = [gather(shelf, 2, peer, 1 + i) for i, peer in enumerate(along)]
    gather_core = gather(core * (2 * n_y), 2 * n_y, mate, n_y)
    for copy in gather_y:
        copy.start()
    for copy in edges[2:]:
        copy.start()
    loads[4].wait()
    lax.fori_loop(0, 2, matmul(own_at, ROW, 2 * D, kv, own_at, D, 512, None), 0)

    def project(starts):
        lax.fori_loop(0, 2, matmul(starts, BT, D, kv, starts, 0, D, None), 0)

    for copy in edges:
        copy.wait_recv()
    for copy in corners:
        copy.start()
    project([BT, BC * BT, bottom + BT, bottom + BC * BT])

    for copy in gather_y:
        copy.wait()
    gather_core.start()
    for copy in half(0, 0):
        copy.start()
    gather_core.wait()
    for copy in half(0, 1) + chunk(1) + sides + chunk(2):
        copy.start()

    one = cells[...].reshape(n_one, D)
    one_hi = one.astype(BF)
    one_lo = (one - one_hi.astype(F32)).astype(BF)
    pick = (
        lax.broadcasted_iota(jnp.int32, (n_two, n_one), 1) // 4
        == lax.broadcasted_iota(jnp.int32, (n_two, n_one), 0)
    ).astype(BF)
    two = jnp.dot(pick, one_hi, preferred_element_type=F32) + jnp.dot(
        pick, one_lo, preferred_element_type=F32
    )
    two_hi = two.astype(BF)
    two_lo = (two - two_hi.astype(F32)).astype(BF)
    sums = jnp.concatenate([one_hi, two_hi, one_lo, two_lo], axis=0)
    same = (
        lax.broadcasted_iota(jnp.int32, (GW, GW), 0) // HD
        == lax.broadcasted_iota(jnp.int32, (GW, GW), 1) // HD
    )
    mean = jnp.where(same, 1.0 / HD, 0.0).astype(BF)

    def pooled(n, carry):
        cols = pl.ds(pl.multiple_of(n * GW, GW), GW)
        wcols = pl.ds(pl.multiple_of(D + n * GW, GW), GW)
        y = jnp.dot(sums, wq[:, wcols], preferred_element_type=F32)
        y = y[:n_far] + y[n_far:]
        sq = jnp.dot((y * y).astype(BF), mean, preferred_element_type=F32)
        far[:, cols] = (y * lax.rsqrt(sq + 1e-5)).astype(BF)
        return carry

    lax.fori_loop(0, 2 * D // GW, pooled, 0)

    lane = lax.broadcasted_iota(jnp.int32, (BT, GW), 1) // HD
    lane_far = lax.broadcasted_iota(jnp.int32, (BT, 128), 1)

    def attend(c):
        items = []
        for r in range(BR):
            corner = r * EXT_ROW + c * BT
            me = corner + EXT_ROW + BT
            b = r * BC + c
            own_id = near_ref[b, 4]
            starts = []
            for j in range(9):
                at = corner + j // 3 * EXT_ROW + j % 3 * BT
                if j in (0, 2, 6, 8):
                    other = near_ref[b, j] - own_id
                    at = me + (at - me) * jnp.minimum(other * other, 1)
                starts.append(at)
            rows = pl.ds(pl.multiple_of(b * BT, BT), BT)
            items += [(rows, starts, g) for g in range(HEADS // GROUP)]

        def scores(rows, starts, g):
            cols = pl.ds(g * GW, GW)
            qb = q[rows, cols]
            zero = jnp.zeros_like(qb)
            qs = jnp.concatenate([jnp.where(lane == h, qb, zero) for h in range(GROUP)], axis=0)
            keys = jnp.concatenate(
                [far[:, cols]] + [kv[pl.ds(at, BT), cols] for at in starts], axis=0
            )
            return lax.dot_general(
                qs, keys, (((1,), (1,)), ((), ())), preferred_element_type=F32
            )

        s_next = scores(*items[0])
        for i, (rows, starts, g) in enumerate(items):
            s = s_next
            if i + 1 < len(items):
                s_next = scores(*items[i + 1])
            add_one = jnp.concatenate(
                [jnp.full((BT, 128), bias_ref[0, g * GROUP + h] * LOG2E, F32) for h in range(GROUP)],
                axis=0,
            )
            add_two = jnp.concatenate(
                [
                    jnp.where(lane_far < n_two, bias_ref[1, g * GROUP + h] * LOG2E, 0.0)
                    for h in range(GROUP)
                ],
                axis=0,
            )
            s = jnp.concatenate(
                [s[:, :128] + add_one, s[:, 128:256] + add_two, s[:, 256:]], axis=1
            )
            p = jnp.exp2(s - jnp.max(s, axis=1, keepdims=True))
            total = jnp.sum(p, axis=1, keepdims=True)
            vcols = pl.ds(D + g * GW, GW)
            vals = jnp.concatenate(
                [far[:, vcols]] + [kv[pl.ds(at, BT), vcols] for at in starts], axis=0
            )
            o = jnp.dot(p.astype(BF), vals, preferred_element_type=F32)
            o = o * (1.0 / total)
            h01 = jnp.where(lane == 0, o[:BT], o[BT : 2 * BT])
            h23 = jnp.where(lane == 2, o[2 * BT : 3 * BT], o[3 * BT :])
            heard[rows, pl.ds(g * GW, GW)] = jnp.where(lane < 2, h01, h23).astype(BF)

    def middle(k, carry):
        for copy in chunk(k):
            copy.wait_recv()
        at = 2 * BT + k * (2 * BT)
        project([at, at + BT, bottom + at, bottom + at + BT])

        def column(c, carry):
            attend(c)
            return carry

        lax.fori_loop(1 + k * (k + 1) // 2, 1 + (k + 1) * (k + 2) // 2, column, 0)
        return carry

    lax.fori_loop(0, 3, middle, 0)

    def outer(i, carry):
        side = core + i - 2 * core * i
        side = 1 - side
        at = side * (9 * BT)
        for row, sem in ((EXT_ROW, 10), (2 * EXT_ROW, 11), (0, 14), (bottom, 15)):
            remote(x_ref, 0, BT, row + at, (face, left), sem + 2 * side).wait_recv()
        project([at, EXT_ROW + at, 2 * EXT_ROW + at, bottom + at])
        attend(side * (BC - 1))
        return carry

    lax.fori_loop(0, 2, outer, 0)

    loads[5].wait()
    stores = []
    for i in range(BR):
        rows = pl.ds(i * ROW, ROW)
        y = jnp.dot(heard[rows, :], wo[...], preferred_element_type=F32)
        mixed[rows, :] = y.astype(BF)
        store = pltpu.make_async_copy(mixed.at[rows], out_ref.at[rows], store_sem.at[i])
        store.start()
        stores.append(store)
    for copy in edges + chunk(0) + chunk(1) + chunk(2) + sides + corners:
        copy.wait_send()
    for store in stores:
        store.wait()


def solution(mesh):
    n_face, n_sub = mesh.shape["face"], mesh.shape["sub"]
    tokens = BR * ROW
    n_far = n_sub * 10

    def body(x, w_qkv, w_out, neighbours, parent_one, parent_two, level_bias):
        call = pl.pallas_call(
            functools.partial(kernel, n_face, n_sub),
            out_shape=jax.ShapeDtypeStruct((tokens, D), BF),
            in_specs=[pl.BlockSpec(memory_space=pl.ANY)] * 3
            + [pl.BlockSpec(memory_space=pltpu.SMEM)] * 2,
            out_specs=pl.BlockSpec(memory_space=pl.ANY),
            scratch_shapes=[
                pltpu.VMEM((EXT, D), BF),
                pltpu.VMEM((D, 3 * D), BF),
                pltpu.VMEM((D, D), BF),
                pltpu.VMEM((tokens, D), BF),
                pltpu.VMEM((EXT, 2 * D), BF),
                pltpu.VMEM((tokens, D), BF),
                pltpu.VMEM((tokens, D), BF),
                pltpu.VMEM((2 * n_face, 2, D), F32),
                pltpu.VMEM((n_sub, 8, D), F32),
                pltpu.VMEM((n_far, 2 * D), BF),
                pltpu.SemaphoreType.DMA((6,)),
                pltpu.SemaphoreType.DMA((BR,)),
                pltpu.SemaphoreType.DMA((18,)),
                pltpu.SemaphoreType.DMA((18,)),
                pltpu.SemaphoreType.DMA((2 * n_face,)),
                pltpu.SemaphoreType.DMA((2 * n_face,)),
                pltpu.SemaphoreType.DMA((n_sub,)),
                pltpu.SemaphoreType.DMA((n_sub,)),
            ],
            compiler_params=pltpu.CompilerParams(
                collective_id=0, has_side_effects=True, vmem_limit_bytes=56 * 1024 * 1024
            ),
            cost_estimate=pl.CostEstimate(
                flops=60_000_000_000, bytes_accessed=16_000_000, transcendentals=12_000_000
            ),
        )
        return call(x, w_qkv, w_out, neighbours, level_bias)

    placed = (
        P(("face", "sub"), None),
        P(),
        P(),
        P(("face", "sub"), None),
        P(("face", "sub")),
        P(),
        P(),
    )
    return jax.shard_map(
        body, mesh=mesh, in_specs=placed, out_specs=P(("face", "sub"), None), check_vma=False
    )
```

```python
import functools

import jax
import jax.numpy as jnp
from jax import lax
from jax.experimental import pallas as pl
from jax.experimental.pallas import tpu as pltpu
from jax.sharding import PartitionSpec as P

D = 1024
HEADS = 16
HD = 64
BT = 64
BR = 2
BC = 8
GROUP = 4
GW = GROUP * HD
WIDE = BC + 2
EXT_ROW = WIDE * BT
EXT = (BR + 2) * EXT_ROW
ROW = BC * BT
LOG2E = 1.4426950408889634
MESH = pl.DeviceIdType.MESH
BF = jnp.bfloat16
F32 = jnp.float32


def kernel(
    n_face,
    n_sub,
    x_ref,
    wqkv_ref,
    near_ref,
    bias_ref,
    out_ref,
    xe,
    wq,
    q,
    kv,
    heard,
    part,
    cells,
    far,
    load_sem,
    store_sem,
    halo_send,
    halo_recv,
    part_send,
    part_recv,
    cell_send,
    cell_recv,
):
    face = lax.axis_index("face")
    sub = lax.axis_index("sub")
    up = lax.rem(face + n_face - 1, n_face)
    down = lax.rem(face + 1, n_face)
    left = lax.rem(sub + n_sub - 1, n_sub)
    right = lax.rem(sub + 1, n_sub)
    n_one = n_sub * 8
    n_two = n_sub * 2
    n_far = n_one + n_two

    core = lax.rem(sub, 2)
    high = lax.rem(sub // 2, 2)
    mate = sub + 1 - 2 * core
    across = sub + 2 - 4 * high
    along = [lax.rem(sub + d, n_sub) for d in range(4, n_sub, 4)]
    n_y = n_sub // 4
    shelf = core * (2 * n_y) + sub // 4 * 2

    peers = [(lax.rem(face + d, n_face), sub) for d in range(1, n_face)]
    peers += [(lax.rem(face + d, n_face), across) for d in range(1, n_face)]
    peers += [(face, left), (face, right), (face, across)] + [(face, far_y) for far_y in along]
    barrier = pltpu.get_barrier_semaphore()
    for peer in peers:
        pl.semaphore_signal(barrier, inc=1, device_id=peer, device_id_type=MESH)

    own = [(EXT_ROW + BT, 0), (2 * EXT_ROW + BT, ROW)]
    loads = []
    for i, (to, at) in enumerate(own):
        loads.append(
            pltpu.make_async_copy(
                x_ref.at[pl.ds(at, ROW)], xe.at[pl.ds(to, ROW)], load_sem.at[i]
            )
        )
    for i in range(3):
        cols = pl.ds(i * D, D)
        loads.append(
            pltpu.make_async_copy(wqkv_ref.at[:, cols], wq.at[:, cols], load_sem.at[2 + i])
        )
    for load in loads:
        load.start()

    loads[0].wait()
    loads[1].wait()
    for half in range(2):
        total = None
        for to, _ in own:
            tok = xe[pl.ds(to + half * (ROW // 2), ROW // 2), :].astype(F32)
            s = jnp.sum(tok, axis=0, keepdims=True)
            total = s if total is None else total + s
        part[high * n_face + face, pl.ds(half, 1), :] = total

    def matmul(row_starts, rows, first, out, out_starts, out_first, width, scale):
        def step(n, carry):
            wcols = pl.ds(pl.multiple_of(first + n * width, width), width)
            cols = pl.ds(pl.multiple_of(out_first + n * width, width), width)
            x = [xe[pl.ds(at, rows), :] for at in row_starts]
            x = x[0] if len(x) == 1 else jnp.concatenate(x, axis=0)
            y = jnp.dot(x, wq[:, wcols], preferred_element_type=F32)
            if scale is not None:
                y = y * scale
            y = y.astype(BF)
            for i, at in enumerate(out_starts):
                out[pl.ds(at, rows), cols] = y[i * rows : (i + 1) * rows]
            return carry

        return step

    own_at = [to for to, _ in own]
    pl.semaphore_wait(barrier, len(peers))

    parts = []
    for d in range(1, 2 * n_face):
        parts.append(
            pltpu.make_async_remote_copy(
                src_ref=part.at[high * n_face + face],
                dst_ref=part.at[high * n_face + face],
                send_sem=part_send.at[d],
                recv_sem=part_recv.at[d],
                device_id=(lax.rem(face + d, n_face), sub if d < n_face else across),
                device_id_type=MESH,
            )
        )
    for copy in parts:
        copy.start()

    def remote(src, src_at, rows, to, peer, i):
        return pltpu.make_async_remote_copy(
            src_ref=src.at[pl.ds(src_at, rows)],
            dst_ref=xe.at[pl.ds(to, rows)],
            send_sem=halo_send.at[i],
            recv_sem=halo_recv.at[i],
            device_id=peer,
            device_id_type=MESH,
        )

    bottom = 3 * EXT_ROW
    last = ROW - BT
    edges = [
        remote(x_ref, 0, BT, bottom + BT, (up, sub), 0),
        remote(x_ref, ROW, BT, BT, (down, sub), 1),
        remote(x_ref, last, BT, bottom + BC * BT, (up, sub), 2),
        remote(x_ref, ROW + last, BT, BC * BT, (down, sub), 3),
    ]

    def chunk(k):
        at = BT + k * (2 * BT)
        return [
            remote(x_ref, at, 2 * BT, bottom + BT + at, (up, sub), 4 + 2 * k),
            remote(x_ref, ROW + at, 2 * BT, BT + at, (down, sub), 5 + 2 * k),
        ]

    def half(k, i):
        at = BT + k * (2 * BT) + i * BT
        return [
            remote(x_ref, at, BT, bottom + BT + at, (up, sub), 4 + 2 * k),
            remote(x_ref, ROW + at, BT, BT + at, (down, sub), 5 + 2 * k),
        ]

    sides = [
        remote(x_ref, last, BT, EXT_ROW, (face, right), 10),
        remote(x_ref, ROW + last, BT, 2 * EXT_ROW, (face, right), 11),
        remote(x_ref, 0, BT, EXT_ROW + 9 * BT, (face, left), 12),
        remote(x_ref, ROW, BT, 2 * EXT_ROW + 9 * BT, (face, left), 13),
    ]
    corners = [
        remote(xe, BC * BT, BT, 0, (face, right), 14),
        remote(xe, bottom + BC * BT, BT, bottom, (face, right), 15),
        remote(xe, BT, BT, 9 * BT, (face, left), 16),
        remote(xe, bottom + BT, BT, bottom + 9 * BT, (face, left), 17),
    ]
    for copy in edges[:2]:
        copy.start()

    loads[2].wait()
    lax.fori_loop(
        0, 2, matmul(own_at, ROW, 0, q, [0, ROW], 0, 512, HD**-0.5 * LOG2E), 0
    )
    loads[3].wait()
    lax.fori_loop(0, 2, matmul(own_at, ROW, D, kv, own_at, 0, 512, None), 0)

    for copy in parts:
        copy.wait()
    for h in range(2):
        for k in range(n_face // 2):
            pair = part[h * n_face + 2 * k] + part[h * n_face + 2 * k + 1]
            cells[shelf + h, pl.ds(2 * k, 2), :] = pair

    def gather(at, count, peer, i):
        return pltpu.make_async_remote_copy(
            src_ref=cells.at[pl.ds(at, count)],
            dst_ref=cells.at[pl.ds(at, count)],
            send_sem=cell_send.at[i],
            recv_sem=cell_recv.at[i],
            device_id=(face, peer),
            device_id_type=MESH,
        )

    gather_y = [gather(shelf, 2, peer, 1 + i) for i, peer in enumerate(along)]
    gather_core = gather(core * (2 * n_y), 2 * n_y, mate, n_y)
    for copy in gather_y:
        copy.start()
    for copy in edges[2:]:
        copy.start()
    loads[4].wait()
    lax.fori_loop(0, 2, matmul(own_at, ROW, 2 * D, kv, own_at, D, 512, None), 0)

    def project(starts):
        lax.fori_loop(0, 2, matmul(starts, BT, D, kv, starts, 0, D, None), 0)

    for copy in edges:
        copy.wait_recv()
    for copy in corners:
        copy.start()
    project([BT, BC * BT, bottom + BT, bottom + BC * BT])

    for copy in gather_y:
        copy.wait()
    gather_core.start()
    for copy in half(0, 0):
        copy.start()
    gather_core.wait()
    for copy in half(0, 1) + chunk(1) + sides + chunk(2):
        copy.start()

    one = cells[...].reshape(n_one, D)
    one_hi = one.astype(BF)
    one_lo = (one - one_hi.astype(F32)).astype(BF)
    pick = (
        lax.broadcasted_iota(jnp.int32, (n_two, n_one), 1) // 4
        == lax.broadcasted_iota(jnp.int32, (n_two, n_one), 0)
    ).astype(BF)
    two = jnp.dot(pick, one_hi, preferred_element_type=F32) + jnp.dot(
        pick, one_lo, preferred_element_type=F32
    )
    two_hi = two.astype(BF)
    two_lo = (two - two_hi.astype(F32)).astype(BF)
    sums = jnp.concatenate([one_hi, two_hi, one_lo, two_lo], axis=0)
    same = (
        lax.broadcasted_iota(jnp.int32, (GW, GW), 0) // HD
        == lax.broadcasted_iota(jnp.int32, (GW, GW), 1) // HD
    )
    mean = jnp.where(same, 1.0 / HD, 0.0).astype(BF)

    def pooled(n, carry):
        width = 2 * GW
        wcols = pl.ds(pl.multiple_of(D + n * width, width), width)
        y = jnp.dot(sums, wq[:, wcols], preferred_element_type=F32)
        y = y[:n_far] + y[n_far:]
        for i in range(2):
            z = y[:, i * GW : (i + 1) * GW]
            sq = jnp.dot((z * z).astype(BF), mean, preferred_element_type=F32)
            cols = pl.ds(pl.multiple_of(n * width + i * GW, GW), GW)
            far[:, cols] = (z * lax.rsqrt(sq + 1e-5)).astype(BF)
        return carry

    lax.fori_loop(0, D // GW, pooled, 0)

    lane = lax.broadcasted_iota(jnp.int32, (BT, GW), 1) // HD
    lane_far = lax.broadcasted_iota(jnp.int32, (BT, 128), 1)

    def store(b):
        rows = pl.ds(pl.multiple_of(b * BT, BT), BT)
        return pltpu.make_async_copy(heard.at[rows], out_ref.at[rows], store_sem.at[b])

    def attend(c):
        items = []
        for r in range(BR):
            corner = r * EXT_ROW + c * BT
            me = corner + EXT_ROW + BT
            b = r * BC + c
            own_id = near_ref[b, 4]
            starts = []
            for j in range(9):
                at = corner + j // 3 * EXT_ROW + j % 3 * BT
                if j in (0, 2, 6, 8):
                    other = near_ref[b, j] - own_id
                    at = me + (at - me) * jnp.minimum(other * other, 1)
                starts.append(at)
            rows = pl.ds(pl.multiple_of(b * BT, BT), BT)
            items += [(rows, starts, g) for g in range(HEADS // GROUP)]

        def scores(rows, starts, g):
            cols = pl.ds(g * GW, GW)
            qb = q[rows, cols]
            zero = jnp.zeros_like(qb)
            qs = jnp.concatenate([jnp.where(lane == h, qb, zero) for h in range(GROUP)], axis=0)
            keys = jnp.concatenate(
                [far[:, cols]] + [kv[pl.ds(at, BT), cols] for at in starts], axis=0
            )
            return lax.dot_general(
                qs, keys, (((1,), (1,)), ((), ())), preferred_element_type=F32
            )

        s_next = scores(*items[0])
        for i, (rows, starts, g) in enumerate(items):
            s = s_next
            if i + 1 < len(items):
                s_next = scores(*items[i + 1])
            add_one = jnp.concatenate(
                [jnp.full((BT, 128), bias_ref[0, g * GROUP + h] * LOG2E, F32) for h in range(GROUP)],
                axis=0,
            )
            add_two = jnp.concatenate(
                [
                    jnp.where(lane_far < n_two, bias_ref[1, g * GROUP + h] * LOG2E, 0.0)
                    for h in range(GROUP)
                ],
                axis=0,
            )
            s = jnp.concatenate(
                [s[:, :128] + add_one, s[:, 128:256] + add_two, s[:, 256:]], axis=1
            )
            p = jnp.exp2(s - jnp.max(s, axis=1, keepdims=True))
            total = jnp.sum(p, axis=1, keepdims=True)
            vcols = pl.ds(D + g * GW, GW)
            vals = jnp.concatenate(
                [far[:, vcols]] + [kv[pl.ds(at, BT), vcols] for at in starts], axis=0
            )
            o = jnp.dot(p.astype(BF), vals, preferred_element_type=F32)
            o = o * (1.0 / total)
            h01 = jnp.where(lane == 0, o[:BT], o[BT : 2 * BT])
            h23 = jnp.where(lane == 2, o[2 * BT : 3 * BT], o[3 * BT :])
            heard[rows, pl.ds(g * GW, GW)] = jnp.where(lane < 2, h01, h23).astype(BF)
        for r in range(BR):
            store(r * BC + c).start()

    def middle(k, carry):
        for copy in chunk(k):
            copy.wait_recv()
        at = 2 * BT + k * (2 * BT)
        project([at, at + BT, bottom + at, bottom + at + BT])

        def column(c, carry):
            attend(c)
            return carry

        lax.fori_loop(1 + k * (k + 1) // 2, 1 + (k + 1) * (k + 2) // 2, column, 0)
        return carry

    lax.fori_loop(0, 3, middle, 0)

    def outer(i, carry):
        side = core + i - 2 * core * i
        side = 1 - side
        at = side * (9 * BT)
        for row, sem in ((EXT_ROW, 10), (2 * EXT_ROW, 11), (0, 14), (bottom, 15)):
            remote(x_ref, 0, BT, row + at, (face, left), sem + 2 * side).wait_recv()
        project([at, EXT_ROW + at, 2 * EXT_ROW + at, bottom + at])
        attend(side * (BC - 1))
        return carry

    lax.fori_loop(0, 2, outer, 0)

    for copy in edges + chunk(0) + chunk(1) + chunk(2) + sides + corners:
        copy.wait_send()
    for b in range(BR * BC):
        store(b).wait()


def out_kernel(heard_ref, w_ref, out_ref):
    out_ref[...] = jnp.dot(heard_ref[...], w_ref[...], preferred_element_type=F32).astype(BF)


def solution(mesh):
    n_face, n_sub = mesh.shape["face"], mesh.shape["sub"]
    tokens = BR * ROW
    n_far = n_sub * 10

    def body(x, w_qkv, w_out, neighbours, parent_one, parent_two, level_bias):
        call = pl.pallas_call(
            functools.partial(kernel, n_face, n_sub),
            out_shape=jax.ShapeDtypeStruct((tokens, D), BF),
            in_specs=[pl.BlockSpec(memory_space=pl.ANY)] * 2
            + [pl.BlockSpec(memory_space=pltpu.SMEM)] * 2,
            out_specs=pl.BlockSpec(memory_space=pl.ANY),
            scratch_shapes=[
                pltpu.VMEM((EXT, D), BF),
                pltpu.VMEM((D, 3 * D), BF),
                pltpu.VMEM((tokens, D), BF),
                pltpu.VMEM((EXT, 2 * D), BF),
                pltpu.VMEM((tokens, D), BF),
                pltpu.VMEM((2 * n_face, 2, D), F32),
                pltpu.VMEM((n_sub, 8, D), F32),
                pltpu.VMEM((n_far, 2 * D), BF),
                pltpu.SemaphoreType.DMA((5,)),
                pltpu.SemaphoreType.DMA((BR * BC,)),
                pltpu.SemaphoreType.DMA((18,)),
                pltpu.SemaphoreType.DMA((18,)),
                pltpu.SemaphoreType.DMA((2 * n_face,)),
                pltpu.SemaphoreType.DMA((2 * n_face,)),
                pltpu.SemaphoreType.DMA((n_sub,)),
                pltpu.SemaphoreType.DMA((n_sub,)),
            ],
            compiler_params=pltpu.CompilerParams(
                collective_id=0, has_side_effects=True, vmem_limit_bytes=56 * 1024 * 1024
            ),
            cost_estimate=pl.CostEstimate(
                flops=60_000_000_000, bytes_accessed=16_000_000, transcendentals=12_000_000
            ),
        )
        heard = call(x, w_qkv, neighbours, level_bias)
        rows = tokens // 4
        return pl.pallas_call(
            out_kernel,
            grid=(4,),
            out_shape=jax.ShapeDtypeStruct((tokens, D), BF),
            in_specs=[
                pl.BlockSpec((rows, D), lambda i: (i, 0)),
                pl.BlockSpec((D, D), lambda i: (0, 0)),
            ],
            out_specs=pl.BlockSpec((rows, D), lambda i: (i, 0)),
            compiler_params=pltpu.CompilerParams(vmem_limit_bytes=32 * 1024 * 1024),
        )(heard, w_out)

    placed = (
        P(("face", "sub"), None),
        P(),
        P(),
        P(("face", "sub"), None),
        P(("face", "sub")),
        P(),
        P(),
    )
    return jax.shard_map(
        body, mesh=mesh, in_specs=placed, out_specs=P(("face", "sub"), None), check_vma=False
    )
```
